32 devices in a mesh: grp: 2 (over y), pan: 4 (over z), seq: 4 (over x, core).
Axes of the slice: x: 2, y: 2, z: 4, core: 2. Of those that a mesh axis runs over, the one named last changes fastest.
Arguments:
- activations: bfloat16 [2048, 8192], P(('grp', 'seq'), 'pan'), parts along dimension 0, may hold values from -6 to 6
- out_grads: bfloat16 [2048, 8192], P(('grp', 'pan'), 'seq'), parts along dimension 0, may hold values from -6 to 6
- act_basis: bfloat16 [16384, 8192], P(('grp', 'pan'), 'seq'), parts along dimension 0, may hold values from -0.0625 to 0.0625
- grad_basis: bfloat16 [16384, 8192], P(('grp', 'seq'), 'pan'), parts along dimension 0, may hold values from -0.0625 to 0.0625
Outputs:
- correction: float32 [16384, 8192], P(('grp', 'pan'), 'seq'), parts along dimension 0
The draws below stay inside these ranges and needn't reach their ends.
There are 2 independent parts, one for each index of `grp`. The reference program is written for one: setup_inputs(seed, part) draws one part's arguments, and reference() takes and returns one part's arrays. A program takes and returns all parts, laid end to end along the dimension named above; each array names one. Nothing has to cross between parts.
All inputs are finite; a program needn't handle non-finite values.
Results may differ from the reference program's by a relative error of at most 0.013.
Values may be sent and summed in bfloat16 or wider, within the bound.
A program may use at most 128 MiB of HBM per device.

```python
import jax
import jax.numpy as jnp
from jax import lax

D = 8192
LEN = 128
SEQS = 8
TOKENS = 1024
PANEL = 2048


def steps_of(rng, dims, shards, smallest, top_value):
    loudness, own = 1.0, jax.random.fold_in(rng, 6)
    for dim, parts in shards:
        draws = jnp.exp(jax.random.uniform(jax.random.fold_in(own, dim), (parts,), jnp.float32, smallest / len(shards), top_value / len(shards)))
        loudness = loudness * jnp.repeat(draws, dims[dim] // parts).reshape([-1 if axis == dim else 1 for axis in range(len(dims))])
    return loudness


def centred(own_key, extent, deviation, reach, pieces=(), kind=jnp.bfloat16):
    drawn = jax.random.normal(own_key, extent, jnp.float32) * deviation
    if len(pieces) > 0:
        drawn = steps_of(own_key, extent, pieces, -0.22, 0.18) * drawn
    return jnp.clip(drawn, min=-reach, max=reach).astype(kind)


def setup_inputs(seed: int = 0, part: int = 0) -> dict:
    splits = jax.random.split(jax.random.key(seed), 5)
    part_splits = jax.random.split(jax.random.fold_in(splits[4], part), 5)
    activations = centred(part_splits[0], (TOKENS, D), 1.0, 6.0, ((0, 4), (1, 4)))
    out_grads = centred(part_splits[1], (TOKENS, D), 1.0, 6.0, ((0, 4), (1, 4)))
    act_basis = centred(part_splits[2], (D, D), D ** -0.5, 0.0625, ((0, 4), (1, 4)))
    grad_basis = centred(part_splits[3], (D, D), D ** -0.5, 0.0625, ((0, 4), (1, 4)))
    return {"activations": activations, "out_grads": out_grads, "act_basis": act_basis, "grad_basis": grad_basis}


def reference(activations, out_grads, act_basis, grad_basis):
    act_panels = activations.reshape(TOKENS, D // PANEL, PANEL).transpose(1, 0, 2)
    basis_panels = act_basis.reshape(D // PANEL, PANEL, D)

    def add_panel(running, operands):
        act_piece, basis_rows = operands
        partial_value = jnp.dot(act_piece, basis_rows, preferred_element_type=jnp.float32)
        rounded = lax.optimization_barrier(partial_value.astype(jnp.bfloat16))
        return running + rounded.astype(jnp.float32), None

    summed = lax.scan(add_panel, jnp.zeros((TOKENS, D), jnp.float32), (act_panels, basis_panels))[0]
    rot_acts = summed.astype(jnp.bfloat16)
    rot_grads = jnp.dot(out_grads, grad_basis, preferred_element_type=jnp.float32).astype(jnp.bfloat16)
    grad_seqs = rot_grads.reshape(SEQS, LEN, D)
    act_seqs = rot_acts.reshape(SEQS, LEN, D)

    def add_sequence(running, operands):
        grad_part, act_part = operands
        grad_block = jnp.dot(grad_part.T, act_part, preferred_element_type=jnp.float32)
        return running + grad_block * grad_block, None

    squares = lax.scan(add_sequence, jnp.zeros((D, D), jnp.float32), (grad_seqs, act_seqs))[0]
    return squares / (SEQS * LEN)
```

```python
import functools

import jax
import jax.numpy as jnp
from jax import lax
from jax.experimental import pallas as pl
from jax.experimental.pallas import tpu as pltpu
from jax.sharding import PartitionSpec as P

LEN = 128
SPLITS = 2


def take(array, index, rows):
    return lax.dynamic_slice_in_dim(array, index * rows, rows, 0)


def add(one, other):
    return (one.astype(jnp.float32) + other.astype(jnp.float32)).astype(one.dtype)


def line_gather(own, axis, n):
    me = lax.axis_index(axis)
    right, left = {}, {}
    going_right = going_left = own
    for t in range(1, n):
        going_right = lax.ppermute(going_right, axis, [(i, i + 1) for i in range(t - 1, n - 1)])
        going_left = lax.ppermute(going_left, axis, [(i, i - 1) for i in range(1, n - t + 1)])
        right[t], left[t] = going_right, going_left
    blocks = [own]
    for t in range(1, n):
        blocks.append(jnp.where(me >= t, right[t], left[n - t]))
    return blocks


def in_order(blocks, axis, n):
    me = lax.axis_index(axis)
    rows = blocks[0].shape[0]
    whole = jnp.zeros((n * rows, blocks[0].shape[1]), blocks[0].dtype)
    for t, block in enumerate(blocks):
        whole = lax.dynamic_update_slice_in_dim(whole, block, lax.rem(me - t + n, n) * rows, 0)
    return whole


def line_reduce_scatter(own, axis, n):
    me = lax.axis_index(axis)
    rows = own.shape[0] // n
    right, left = take(own, me + n - 1, rows), take(own, me - n + 1, rows)
    for d in range(n - 1, 0, -1):
        right = lax.ppermute(right, axis, [(i, i + 1) for i in range(n - d)])
        left = lax.ppermute(left, axis, [(i, i - 1) for i in range(d, n)])
        if d > 1:
            right = add(right, take(own, me - 1 + d, rows))
            left = add(left, take(own, me + 1 - d, rows))
    total = take(own, me, rows).astype(jnp.float32)
    return (total + right.astype(jnp.float32) + left.astype(jnp.float32)).astype(own.dtype)


def squares_kernel(sequences, tile, scale, grads_ref, acts_ref, out_ref):
    for column in range(0, out_ref.shape[1], tile):
        columns = pl.ds(column, tile)
        total = None
        for s in range(sequences):
            block = jnp.dot(
                grads_ref[:, pl.ds(s * LEN, LEN)],
                acts_ref[pl.ds(s * LEN, LEN), columns],
                preferred_element_type=jnp.float32,
            )
            total = block * block if total is None else total + block * block
        out_ref[:, columns] = total * scale


def squares(grads_t, acts):
    rows, tokens = grads_t.shape
    cols = acts.shape[1]
    step = min(256, rows)
    return pl.pallas_call(
        functools.partial(squares_kernel, tokens // LEN, min(512, cols), 1.0 / tokens),
        grid=(rows // step,),
        in_specs=[
            pl.BlockSpec((step, tokens), lambda i: (i, 0)),
            pl.BlockSpec((tokens, cols), lambda i: (0, 0)),
        ],
        out_specs=pl.BlockSpec((step, cols), lambda i: (i, 0)),
        out_shape=jax.ShapeDtypeStruct((rows, cols), jnp.float32),
        compiler_params=pltpu.CompilerParams(vmem_limit_bytes=40 * 1024 * 1024),
        cost_estimate=pl.CostEstimate(
            flops=2 * rows * cols * tokens,
            bytes_accessed=4 * rows * cols + 2 * tokens * (rows + cols),
            transcendentals=0,
        ),
    )(grads_t, acts)


def per_device(pan, activations, out_grads, act_basis, grad_basis):
    full_acts = lax.all_gather(activations, "seq", axis=0, tiled=True)
    full_grads = in_order(line_gather(out_grads, "pan", pan), "pan", pan)
    tokens = full_acts.shape[0]
    part = tokens // SPLITS
    act_parts = []
    for k in range(SPLITS):
        terms = jnp.dot(
            full_acts[k * part : (k + 1) * part], act_basis, preferred_element_type=jnp.float32
        ).astype(jnp.bfloat16)
        mine = line_reduce_scatter(terms, "pan", pan)
        act_parts.append(in_order(line_gather(mine, "pan", pan), "pan", pan))
    rot_acts = jnp.concatenate(act_parts, 0)
    terms_t = lax.dot_general(
        grad_basis, full_grads, (((0,), (1,)), ((), ())), preferred_element_type=jnp.float32
    ).astype(jnp.bfloat16)
    rot_grads_t = lax.psum(terms_t, "seq")
    return squares(rot_grads_t, rot_acts)


def solution(mesh):
    return jax.shard_map(
        functools.partial(per_device, mesh.shape["pan"]),
        mesh=mesh,
        in_specs=(
            P(("grp", "seq"), "pan"),
            P(("grp", "pan"), "seq"),
            P(("grp", "pan"), "seq"),
            P(("grp", "seq"), "pan"),
        ),
        out_specs=P(("grp", "pan"), "seq"),
        check_vma=False,
    )
```

```python
import functools

import jax
import jax.numpy as jnp
from jax import lax
from jax.experimental import pallas as pl
from jax.experimental.pallas import tpu as pltpu
from jax.sharding import PartitionSpec as P

LEN = 128
SPLITS = 2


def take(array, index, rows):
    return lax.dynamic_slice_in_dim(array, index * rows, rows, 0)


def add(one, other):
    return (one.astype(jnp.float32) + other.astype(jnp.float32)).astype(one.dtype)


def line_gather(own, axis, n, ready=()):
    me = lax.axis_index(axis)
    right, left = {}, {}
    going_right = going_left = own
    for t in range(1, n):
        going_right = lax.ppermute(going_right, axis, [(i, i + 1) for i in range(t - 1, n - 1)])
        going_left = lax.ppermute(going_left, axis, [(i, i - 1) for i in range(1, n - t + 1)])
        if t == 2 and ready:
            going_right, going_left, ready = lax.optimization_barrier((going_right, going_left, ready))
        right[t], left[t] = going_right, going_left
    blocks = [own]
    for t in range(1, n):
        blocks.append(jnp.where(me >= t, right[t], left[n - t]))
    return blocks, ready


def in_order(blocks, axis, n):
    me = lax.axis_index(axis)
    rows = blocks[0].shape[0]
    whole = jnp.zeros((n * rows, blocks[0].shape[1]), blocks[0].dtype)
    for t, block in enumerate(blocks):
        whole = lax.dynamic_update_slice_in_dim(whole, block, lax.rem(me - t + n, n) * rows, 0)
    return whole


def line_reduce_scatter(own, axis, n, pin, when):
    me = lax.axis_index(axis)
    rows = own.shape[0] // n
    right, left = take(own, me + n - 1, rows), take(own, me - n + 1, rows)
    for d in range(n - 1, 0, -1):
        right = lax.ppermute(right, axis, [(i, i + 1) for i in range(n - d)])
        left = lax.ppermute(left, axis, [(i, i - 1) for i in range(d, n)])
        if d == when and pin is not None:
            right, left, pin = lax.optimization_barrier((right, left, pin))
        if d > 1:
            right = add(right, take(own, me - 1 + d, rows))
            left = add(left, take(own, me + 1 - d, rows))
    total = take(own, me, rows).astype(jnp.float32)
    return (total + right.astype(jnp.float32) + left.astype(jnp.float32)).astype(own.dtype), pin


def squares_kernel(sequences, tile, scale, *refs):
    grads_ref, acts_ref, *before, out_ref = refs
    for column in range(0, out_ref.shape[1], tile):
        columns = pl.ds(column, tile)
        total = None
        for s in range(sequences):
            block = jnp.dot(
                grads_ref[:, pl.ds(s * LEN, LEN)],
                acts_ref[pl.ds(s * LEN, LEN), columns],
                preferred_element_type=jnp.float32,
            )
            total = block * block if total is None else total + block * block
        total = total * scale
        out_ref[:, columns] = before[0][:, columns] + total if before else total


def squares(grads_t, acts, k, before):
    rows, tokens = grads_t.shape
    part, cols = acts.shape
    step = min(256, rows)
    out_spec = pl.BlockSpec((step, cols), lambda i: (i, 0))
    return pl.pallas_call(
        functools.partial(squares_kernel, part // LEN, min(512, cols), 1.0 / tokens),
        grid=(rows // step,),
        in_specs=[
            pl.BlockSpec((step, part), lambda i: (i, k)),
            pl.BlockSpec((part, cols), lambda i: (0, 0)),
        ]
        + [out_spec] * len(before),
        out_specs=out_spec,
        out_shape=jax.ShapeDtypeStruct((rows, cols), jnp.float32),
        input_output_aliases={2: 0} if before else {},
        compiler_params=pltpu.CompilerParams(vmem_limit_bytes=40 * 1024 * 1024),
        cost_estimate=pl.CostEstimate(
            flops=4 * rows * cols * part,
            bytes_accessed=4 * rows * cols * (1 + len(before)) + 2 * part * (rows + cols),
            transcendentals=0,
        ),
    )(grads_t, acts, *before)


def rotate_t(blocks, basis):
    rows = jnp.concatenate(blocks, 0)
    return lax.dot_general(
        basis, rows, (((0,), (1,)), ((), ())), preferred_element_type=jnp.float32
    ).astype(jnp.bfloat16)


def per_device(pan, activations, out_grads, act_basis, grad_basis):
    full_acts = lax.all_gather(activations, "seq", axis=0, tiled=True)
    tokens = full_acts.shape[0]
    part = tokens // SPLITS
    act_terms = [
        jnp.dot(
            full_acts[k * part : (k + 1) * part], act_basis, preferred_element_type=jnp.float32
        ).astype(jnp.bfloat16)
        for k in range(SPLITS)
    ]
    blocks, _ = line_gather(out_grads, "pan", pan, act_terms)
    by_arrival = sorted(range(pan), key=lambda t: (max(t, pan - t) if t else 0, t))
    groups = [by_arrival[: pan // 2], by_arrival[pan // 2 :]]
    terms_t = [rotate_t([blocks[t] for t in group], grad_basis) for group in groups]

    act_parts = []
    for k, terms in enumerate(act_terms):
        pin = terms_t[k] if k < 2 else None
        mine, pin = line_reduce_scatter(terms, "pan", pan, pin, pan - 1 - k)
        if k < 2:
            terms_t[k] = pin
        act_parts.append(mine)
    act_parts = [in_order(line_gather(mine, "pan", pan)[0], "pan", pan) for mine in act_parts]

    rows = out_grads.shape[0]
    me = lax.axis_index("pan")
    rot_grads_t = jnp.zeros((grad_basis.shape[1], tokens), jnp.bfloat16)
    first = lax.psum(terms_t[0], "seq")
    first, late = lax.optimization_barrier((first, terms_t[1]))
    for group, sums in zip(groups, [first, lax.psum(late, "seq")]):
        for place, t in enumerate(group):
            rot_grads_t = lax.dynamic_update_slice_in_dim(
                rot_grads_t,
                sums[:, place * rows : (place + 1) * rows],
                lax.rem(me - t + pan, pan) * rows,
                1,
            )
    out = []
    for k, acts in enumerate(act_parts):
        out = [squares(rot_grads_t, acts, k, out)]
    return out[0]


def solution(mesh):
    return jax.shard_map(
        functools.partial(per_device, mesh.shape["pan"]),
        mesh=mesh,
        in_specs=(
            P(("grp", "seq"), "pan"),
            P(("grp", "pan"), "seq"),
            P(("grp", "pan"), "seq"),
            P(("grp", "seq"), "pan"),
        ),
        out_specs=P(("grp", "pan"), "seq"),
        check_vma=False,
    )
```

```python
import functools

import jax
import jax.numpy as jnp
from jax import lax
from jax.experimental import pallas as pl
from jax.experimental.pallas import tpu as pltpu
from jax.sharding import PartitionSpec as P

LEN = 128
SPLITS = 2


def take(array, index, rows):
    return lax.dynamic_slice_in_dim(array, index * rows, rows, 0)


def add(one, other):
    return (one.astype(jnp.float32) + other.astype(jnp.float32)).astype(one.dtype)


def line_gather(own, axis, n, ready=()):
    me = lax.axis_index(axis)
    right, left = {}, {}
    going_right = going_left = own
    for t in range(1, n):
        going_right = lax.ppermute(going_right, axis, [(i, i + 1) for i in range(t - 1, n - 1)])
        going_left = lax.ppermute(going_left, axis, [(i, i - 1) for i in range(1, n - t + 1)])
        if t == 2 and ready:
            going_right, going_left, ready = lax.optimization_barrier((going_right, going_left, ready))
        right[t], left[t] = going_right, going_left
    blocks = [own]
    for t in range(1, n):
        blocks.append(jnp.where(me >= t, right[t], left[n - t]))
    return blocks, ready


def in_order(blocks, axis, n):
    me = lax.axis_index(axis)
    rows = blocks[0].shape[0]
    whole = jnp.zeros((n * rows, blocks[0].shape[1]), blocks[0].dtype)
    for t, block in enumerate(blocks):
        whole = lax.dynamic_update_slice_in_dim(whole, block, lax.rem(me - t + n, n) * rows, 0)
    return whole


def line_reduce_scatter(own, axis, n, pin, when):
    me = lax.axis_index(axis)
    rows = own.shape[0] // n
    right, left = take(own, me + n - 1, rows), take(own, me - n + 1, rows)
    for d in range(n - 1, 0, -1):
        right = lax.ppermute(right, axis, [(i, i + 1) for i in range(n - d)])
        left = lax.ppermute(left, axis, [(i, i - 1) for i in range(d, n)])
        if d == when and pin is not None:
            right, left, pin = lax.optimization_barrier((right, left, pin))
        if d > 1:
            right = add(right, take(own, me - 1 + d, rows))
            left = add(left, take(own, me + 1 - d, rows))
    total = take(own, me, rows).astype(jnp.float32)
    return (total + right.astype(jnp.float32) + left.astype(jnp.float32)).astype(own.dtype), pin


def squares_kernel(tile, scale, grads_ref, *refs):
    *parts, out_ref = refs
    part = parts[0].shape[0]
    for column in range(0, out_ref.shape[1], tile):
        columns = pl.ds(column, tile)
        total = None
        for k, acts_ref in enumerate(parts):
            for s in range(0, part, LEN):
                block = jnp.dot(
                    grads_ref[:, pl.ds(k * part + s, LEN)],
                    acts_ref[pl.ds(s, LEN), columns],
                    preferred_element_type=jnp.float32,
                )
                total = block * block if total is None else total + block * block
        out_ref[:, columns] = total * scale


def squares(grads_t, act_parts):
    rows, tokens = grads_t.shape
    part, cols = act_parts[0].shape
    step = min(256, rows)
    return pl.pallas_call(
        functools.partial(squares_kernel, min(512, cols), 1.0 / tokens),
        grid=(rows // step,),
        in_specs=[pl.BlockSpec((step, tokens), lambda i: (i, 0))]
        + [pl.BlockSpec((part, cols), lambda i: (0, 0))] * len(act_parts),
        out_specs=pl.BlockSpec((step, cols), lambda i: (i, 0)),
        out_shape=jax.ShapeDtypeStruct((rows, cols), jnp.float32),
        compiler_params=pltpu.CompilerParams(vmem_limit_bytes=40 * 1024 * 1024),
        cost_estimate=pl.CostEstimate(
            flops=4 * rows * cols * tokens,
            bytes_accessed=4 * rows * cols + 2 * tokens * (rows + cols),
            transcendentals=0,
        ),
    )(grads_t, *act_parts)


def rotate_t(blocks, basis):
    rows = jnp.concatenate(blocks, 0)
    return lax.dot_general(
        basis, rows, (((0,), (1,)), ((), ())), preferred_element_type=jnp.float32
    ).astype(jnp.bfloat16)


def per_device(pan, activations, out_grads, act_basis, grad_basis):
    full_acts = lax.all_gather(activations, "seq", axis=0, tiled=True)
    tokens = full_acts.shape[0]
    part = tokens // SPLITS
    act_terms = [
        jnp.dot(
            full_acts[k * part : (k + 1) * part], act_basis, preferred_element_type=jnp.float32
        ).astype(jnp.bfloat16)
        for k in range(SPLITS)
    ]
    blocks, _ = line_gather(out_grads, "pan", pan, act_terms)
    by_arrival = sorted(range(pan), key=lambda t: (max(t, pan - t) if t else 0, t))
    groups = [by_arrival[: pan // 2], by_arrival[pan // 2 :]]
    terms_t = [rotate_t([blocks[t] for t in group], grad_basis) for group in groups]

    act_parts = []
    for k, terms in enumerate(act_terms):
        pin = terms_t[k] if k < 2 else None
        mine, pin = line_reduce_scatter(terms, "pan", pan, pin, pan - 1 - k)
        if k < 2:
            terms_t[k] = pin
        act_parts.append(mine)
    act_parts = [in_order(line_gather(mine, "pan", pan)[0], "pan", pan) for mine in act_parts]

    rows = out_grads.shape[0]
    me = lax.axis_index("pan")
    rot_grads_t = jnp.zeros((grad_basis.shape[1], tokens), jnp.bfloat16)
    first = lax.psum(terms_t[0], "seq")
    first, late = lax.optimization_barrier((first, terms_t[1]))
    second, act_parts = lax.optimization_barrier((lax.psum(late, "seq"), act_parts))
    for group, sums in zip(groups, [first, second]):
        for place, t in enumerate(group):
            rot_grads_t = lax.dynamic_update_slice_in_dim(
                rot_grads_t,
                sums[:, place * rows : (place + 1) * rows],
                lax.rem(me - t + pan, pan) * rows,
                1,
            )
    return squares(rot_grads_t, act_parts)


def solution(mesh):
    return jax.shard_map(
        functools.partial(per_device, mesh.shape["pan"]),
        mesh=mesh,
        in_specs=(
            P(("grp", "seq"), "pan"),
            P(("grp", "pan"), "seq"),
            P(("grp", "pan"), "seq"),
            P(("grp", "seq"), "pan"),
        ),
        out_specs=P(("grp", "pan"), "seq"),
        check_vma=False,
    )
```
